32 devices in a mesh: section: 2 (over core), seq: 4 (over z), wt: 4 (over y, x).
Axes of the slice: x: 2, y: 2, z: 4, core: 2. Of those that a mesh axis runs over, the one named last changes fastest.
Arguments:
- block_input: bfloat16 [2, 4, 256, 1024], P(None, 'wt', 'seq'), may hold values from -6 to 6
- positions: int32 [2, 4, 256], P(None, 'wt', 'seq'), may hold values from 0 to 255, as said below
- cotangent: bfloat16 [2, 4, 256, 1024], P(None, 'wt', 'seq'), may hold values from -6 to 6
- norm_gain: float32 [2, 1024], P('section'), may hold values from 0.5 to 1.5
- in_weight: bfloat16 [2, 1024, 4384], P('section', 'wt'), may hold values from -0.1875 to 0.1875
- conv_weight: float32 [2, 4, 2304], P('section'), may hold values from -3 to 3
- conv_bias: float32 [2, 2304], P('section'), may hold values from -3 to 3
- dt_bias: float32 [2, 32], P('section'), may hold values from -9 to -3
- a_log: float32 [2, 32], P('section'), may hold values from -2.3 to 1
- skip_d: float32 [2, 32], P('section'), may hold values from 0.5 to 1.5
- gate_gain: float32 [2, 2048], P('section'), may hold values from 0.5 to 1.5
- out_weight: bfloat16 [2, 2048, 1024], P('section', 'wt'), may hold values from -0.125 to 0.125
Outputs:
- section_out: bfloat16 [2, 2, 4, 256, 1024], P('section', None, 'wt', 'seq')
- input_grad: float32 [2, 2, 4, 256, 1024], P('section', None, 'wt', 'seq')
- grad_norm_gain: float32 [2, 1024], P('section')
- grad_in_weight: float32 [2, 1024, 4384], P('section', 'wt')
- grad_conv_weight: float32 [2, 4, 2304], P('section')
- grad_conv_bias: float32 [2, 2304], P('section')
- grad_dt_bias: float32 [2, 32], P('section')
- grad_a_log: float32 [2, 32], P('section')
- grad_skip_d: float32 [2, 32], P('section')
- grad_gate_gain: float32 [2, 2048], P('section')
- grad_out_weight: float32 [2, 2048, 1024], P('section', 'wt')
The draws below stay inside these ranges and needn't reach their ends.
Inputs may be any that keep to these rules, and one draw needn't show every extreme that they name: `positions`: each row begins a document at its first token and holds one to three documents; a position counts the tokens before it in its document. Some row holds a single document.
All inputs are finite; a program needn't handle non-finite values.
Results may differ from the reference program's by a relative error of at most 0.018.
Values may be sent and summed in bfloat16 or wider, within the bound.
A program may use at most 192 MiB of HBM per device.

```python
import jax
import jax.numpy as jnp
from jax import lax

D = 1024
H = 32
P_SIZE = 64
N = 128
K = 4
SPAN = 256
MB = 2
DI = 2048
CH = 2304
E = 4384
CTX = 256
ROWS = 4


def draw_positions(key, part):
    key = jax.random.fold_in(key, 11)
    keys = jax.random.split(key, 5)
    count = MB * ROWS
    first_cut = jax.random.randint(keys[0], (count, 1), CTX // 8, 3 * CTX // 8)
    second_cut = jax.random.randint(keys[1], (count, 1), 5 * CTX // 8, 7 * CTX // 8)
    use_first = jax.random.randint(keys[2], (count, 1), 0, 2)
    use_second = jax.random.randint(keys[3], (count, 1), 0, 2)
    whole_row = jax.random.randint(keys[4], (), 0, count)
    single = (lax.iota(jnp.int32, count) == whole_row)[:, None]
    use_first = jnp.where(single, 0, use_first)
    use_second = jnp.where(single, 0, use_second)
    indices = lax.iota(jnp.int32, CTX)[None, :]
    begins = jnp.where((use_first == 1) & (indices >= first_cut), first_cut, 0)
    begins = jnp.where((use_second == 1) & (indices >= second_cut), second_cut, begins)
    return (indices - begins).reshape(MB, ROWS, CTX).astype(jnp.int32)


def block_scale(stream_key, dims, shards, least, high):
    level = 1.0
    for dim, parts in shards:
        heights = jax.random.uniform(jax.random.fold_in(jax.random.fold_in(stream_key, 6), dim), (parts,), jnp.float32, least / len(shards), high / len(shards))
        level = level * jnp.repeat(jnp.exp(heights), dims[dim] // parts).reshape((-1,) + (1,) * (len(dims) - 1 - dim))
    return level


def scatter_about(rng, shape, scale, reach, pieces=(), kind=jnp.bfloat16):
    values = scale * jax.random.normal(rng, shape, jnp.float32)
    if pieces:
        values = values * block_scale(rng, shape, pieces, -0.22, 0.18)
    return jnp.clip(values, -reach, reach).astype(kind)


def setup_inputs(seed: int = 0) -> dict:
    arg_keys = jax.random.split(jax.random.key(seed), 13)
    return {
        "block_input": scatter_about(arg_keys[0], (MB, ROWS, CTX, D), 1.0, 6.0, ((1, 4), (2, 4))),
        "positions": draw_positions(jax.random.fold_in(arg_keys[12], 71), 0),
        "cotangent": scatter_about(arg_keys[2], (MB, ROWS, CTX, D), 1.0, 6.0, ((1, 4), (2, 4))),
        "norm_gain": jnp.clip(1.0 + 0.1 * jax.random.normal(arg_keys[3], (2, D), jnp.float32), 0.5, 1.5),
        "in_weight": scatter_about(arg_keys[4], (2, D, E), D ** -0.5, 0.1875, ((0, 2), (1, 4))),
        "conv_weight": scatter_about(arg_keys[5], (2, K, CH), K ** -0.5, 3.0, ((0, 2),), jnp.float32),
        "conv_bias": scatter_about(arg_keys[6], (2, CH), 0.5, 3.0, ((0, 2),), jnp.float32),
        "dt_bias": jnp.clip(-9.0 + 6.0 * jax.random.uniform(arg_keys[7], (2, H), jnp.float32) ** block_scale(arg_keys[7], (2, H), ((0, 2),), -0.2, 0.2), -9.0, -3.0),
        "a_log": jnp.clip(-2.3 + 3.3 * jax.random.uniform(arg_keys[8], (2, H), jnp.float32) ** block_scale(arg_keys[8], (2, H), ((0, 2),), -0.2, 0.2), -2.3, 1.0),
        "skip_d": jnp.clip(0.5 + 1.0 * jax.random.uniform(arg_keys[9], (2, H), jnp.float32) ** block_scale(arg_keys[9], (2, H), ((0, 2),), -0.2, 0.2), 0.5, 1.5),
        "gate_gain": jnp.clip(1.0 + 0.1 * jax.random.normal(arg_keys[10], (2, DI), jnp.float32), 0.5, 1.5),
        "out_weight": scatter_about(arg_keys[11], (2, DI, D), DI ** -0.5, 0.125, ((0, 2), (1, 4))),
    }


EPSILON = 1e-05
HIGHEST = lax.Precision.HIGHEST

@jax.custom_vjp
def low(v):
    return lax.optimization_barrier(v.astype(jnp.bfloat16)).astype(jnp.float32)

@jax.custom_vjp
def low_back(v):
    return v

def low_keep(v):
    return (low(v), None)

def low_pass(kept, grad):
    return (grad,)

def back_keep(v):
    return (v, None)

def back_low(kept, grad):
    return (low(grad),)
low.defvjp(low_keep, low_pass)
low_back.defvjp(back_keep, back_low)

def swish(value):
    return value * jax.nn.sigmoid(value)

def lagged(channels, offset):
    return jnp.concatenate([jnp.zeros((offset, channels.shape[1]), channels.dtype), channels[:-offset]], 0)

def convolve(channels, weights, biases, places):
    total = biases + channels * weights[0]
    for offset in range(1, K):
        total = total + jnp.where((places >= offset)[:, None], lagged(channels, offset) * weights[offset], 0.0)
    return total

def scan_heads(x_conv, steps, rates, skips, b_conv, c_conv, doc_start):
    spans = CTX // SPAN
    starts = doc_start.reshape(spans, SPAN)
    inside = jnp.arange(SPAN, dtype=jnp.int32)
    causal = (inside[:, None] >= inside[None, :])[None] & (starts[:, :, None] == starts[:, None, :])
    at_end = starts == starts[:, -1:]
    at_start = starts == starts[:, :1]
    blocks = jnp.arange(spans, dtype=jnp.int32)
    between = ((blocks[None, :, None] < blocks[None, None, :]) & (blocks[None, None, :] < blocks[:, None, None])).astype(x_conv.dtype)
    across = (starts[None, :, -1] == starts[:, 0][:, None]) & (blocks[None, :] < blocks[:, None])
    b_blocks = b_conv.reshape(spans, SPAN, N)
    c_blocks = c_conv.reshape(spans, SPAN, N)
    scores = low_back(jnp.einsum('cln,csn->cls', c_blocks, b_blocks, precision=HIGHEST))

    def one_head(item):
        x_head, step_head, rate, skip = item
        cumul = jnp.cumsum(step_head * rate, axis=1)
        spread = cumul[:, :, None] - cumul[:, None, :]
        decay = jnp.where(causal, jnp.exp(jnp.where(causal, spread, 0.0)), 0.0)
        weights = low(scores * decay * step_head[:, None, :])
        local = jnp.einsum('cls,csp->clp', weights, x_head, precision=HIGHEST)
        tail = jnp.where(at_end, jnp.exp(cumul[:, -1:] - cumul), 0.0)
        inflow = low(x_head * (step_head * tail)[:, :, None])
        state = low_back(jnp.einsum('csn,csp->cnp', b_blocks, inflow, precision=HIGHEST))
        segment = jnp.einsum('k,cdk->cd', cumul[:, -1], between, precision=HIGHEST)
        mixing = jnp.where(across, jnp.exp(jnp.where(across, segment, 0.0)), 0.0)
        carried = low(jnp.einsum('cd,dnp->cnp', mixing, state, precision=HIGHEST))
        readout = low_back(jnp.einsum('cln,cnp->clp', c_blocks, carried, precision=HIGHEST))
        leading = jnp.where(at_start, jnp.exp(cumul), 0.0)
        return local + readout * leading[:, :, None] + skip * x_head
    x_heads = x_conv.reshape(spans, SPAN, H, P_SIZE).transpose(2, 0, 1, 3)
    step_heads = steps.reshape(spans, SPAN, H).transpose(2, 0, 1)
    result = lax.map(jax.checkpoint(one_head), (x_heads, step_heads, rates, skips))
    return result.transpose(1, 2, 0, 3).reshape(CTX, DI)

def block(section_in, places, params):
    gain, w_in, conv_w, conv_b, step_bias, rate_log, skips, gate, w_out = params
    normed = low(section_in * lax.rsqrt(lax.optimization_barrier(jnp.mean(section_in * section_in, axis=-1, keepdims=True)) + EPSILON) * gain)
    proj = low_back(jnp.dot(normed, w_in, precision=HIGHEST))
    z_gate = proj[:, :DI]
    sent = low(proj[:, DI:])
    act = low(swish(convolve(sent[:, :CH], conv_w, conv_b, places)))
    steps = jax.nn.softplus(sent[:, CH:] + step_bias)
    doc_start = jnp.arange(CTX, dtype=jnp.int32) - places
    mixed = scan_heads(act[:, :DI], steps, -jnp.exp(rate_log), skips, act[:, DI:DI + N], act[:, DI + N:], doc_start)
    y_tok = low(low_back(mixed))
    gated = y_tok * swish(z_gate)
    nrm = low(gated * lax.rsqrt(lax.optimization_barrier(jnp.mean(gated * gated, axis=-1, keepdims=True)) + EPSILON) * gate)
    return section_in + low_back(jnp.dot(nrm, w_out, precision=HIGHEST))

def reference(block_input, positions, cotangent, norm_gain, in_weight, conv_weight, conv_bias, dt_bias, a_log, skip_d, gate_gain, out_weight):
    stacks = (norm_gain, in_weight, conv_weight, conv_bias, dt_bias, a_log, skip_d, gate_gain, out_weight)
    first = tuple((item[0].astype(jnp.float32) for item in stacks))
    second = tuple((item[1].astype(jnp.float32) for item in stacks))
    rows_in = block_input.reshape(MB * ROWS, CTX, D)
    rows_pos = positions.reshape(MB * ROWS, CTX)
    rows_cot = cotangent.reshape(MB * ROWS, CTX, D)

    def row_step(totals, item):
        row_in, row_pos, row_cot = item
        start_value = row_in.astype(jnp.float32)
        out_first, back_first = jax.vjp(lambda value, params: block(value, row_pos, params), start_value, first)
        middle = low(out_first)
        out_second, back_second = jax.vjp(lambda value, params: block(value, row_pos, params), middle, second)
        grad_middle, grads_second = back_second(row_cot.astype(jnp.float32))
        grad_start, grads_first = back_first(grad_middle)
        totals = (jax.tree.map(jnp.add, totals[0], grads_first), jax.tree.map(jnp.add, totals[1], grads_second))
        return (totals, (middle.astype(jnp.bfloat16), out_second.astype(jnp.bfloat16), grad_start, grad_middle))
    zeros = (jax.tree.map(jnp.zeros_like, first), jax.tree.map(jnp.zeros_like, second))
    totals, (mid_rows, final_rows, grad_first_rows, grad_second_rows) = lax.scan(row_step, zeros, (rows_in, rows_pos, rows_cot))
    section_out = jnp.stack([mid_rows, final_rows]).reshape(2, MB, ROWS, CTX, D)
    input_grad = jnp.stack([grad_first_rows, grad_second_rows]).reshape(2, MB, ROWS, CTX, D)
    grads = tuple((jnp.stack([left, right]) for left, right in zip(totals[0], totals[1])))
    return (section_out, input_grad, grads[0], grads[1], grads[2], grads[3], grads[4], grads[5], grads[6], grads[7], grads[8])
```

```python
import functools

import jax
import jax.numpy as jnp
from jax import lax
from jax.experimental import pallas as pl
from jax.experimental.pallas import tpu as pltpu
from jax.sharding import PartitionSpec as P

H = 32
P_SIZE = 64
N = 128
K = 4
SPAN = 256
DI = 2048


EPSILON = 1e-05
HIGHEST = lax.Precision.HIGHEST
CONTRACT_ROWS = (((0,), (0,)), ((), ()))
CONTRACT_COLS = (((1,), (1,)), ((), ()))


def from_behind(block, axis, distance):
    devices = range(lax.axis_size(axis))
    route = [(i - distance, i) for i in devices if i - distance in devices]
    return lax.ppermute(block, axis, route)


def swish_slope(value):
    sigma = jax.nn.sigmoid(value)
    return sigma * (1.0 + value * (1.0 - sigma))


def lagged(channels, offset):
    return jnp.concatenate(
        [jnp.zeros((offset, channels.shape[1]), channels.dtype), channels[:-offset]], 0
    )


def leading_rows(channels, offset):
    return jnp.concatenate(
        [channels[offset:], jnp.zeros((offset, channels.shape[1]), channels.dtype)], 0
    )


def convolve(channels, weights, biases, places):
    values = channels.astype(jnp.float32)
    total = biases + values * weights[0]
    for offset in range(1, weights.shape[0]):
        total = total + jnp.where(
            (places >= offset)[:, None], lagged(values, offset) * weights[offset], 0.0
        )
    return total


def convolve_back(grad_pre, channels, weights, places):
    values = channels.astype(jnp.float32)
    weight_rows = [jnp.sum(grad_pre * values, axis=0)]
    grad_chan = grad_pre * weights[0]
    for offset in range(1, weights.shape[0]):
        masked = jnp.where((places >= offset)[:, None], grad_pre, 0.0)
        weight_rows.append(jnp.sum(masked * lagged(values, offset), axis=0))
        grad_chan = grad_chan + leading_rows(masked * weights[offset], offset)
    return (grad_chan, jnp.stack(weight_rows), jnp.sum(grad_pre, axis=0))


def block_tables(doc_start):
    spans = doc_start.shape[0] // SPAN
    starts = doc_start.reshape(spans, SPAN)
    inside = lax.iota(jnp.int32, SPAN)
    causal = (inside[:, None] >= inside[None, :])[None] & (starts[:, :, None] == starts[:, None, :])
    at_end = starts == starts[:, -1:]
    at_start = starts == starts[:, :1]
    blocks = lax.iota(jnp.int32, spans)
    between = (
        (blocks[None, :, None] < blocks[None, None, :])
        & (blocks[None, None, :] < blocks[:, None, None])
    ).astype(jnp.float32)
    across = (starts[None, :, -1] == starts[:, 0][:, None]) & (blocks[None, :] < blocks[:, None])
    return (causal, at_end, at_start, between, across)


def scan_values(x_blocks, b_blocks, c_blocks, step_heads, rates, tables):
    causal, at_end, at_start, between, across = tables
    cumul = jnp.cumsum(step_heads * rates[None, :, None], axis=2)
    spread = cumul[:, :, :, None] - cumul[:, :, None, :]
    inner_mask = causal[:, None]
    decay = jnp.where(inner_mask, jnp.exp(jnp.where(inner_mask, spread, 0.0)), 0.0)
    tail = jnp.where(at_end[:, None], jnp.exp(cumul[:, :, -1:] - cumul), 0.0)
    leading = jnp.where(at_start[:, None], jnp.exp(cumul), 0.0)
    segment = jnp.einsum("kh,cdk->hcd", cumul[:, :, -1], between, precision=HIGHEST)
    mixing = jnp.where(across[None], jnp.exp(jnp.where(across[None], segment, 0.0)), 0.0)
    scores = jnp.einsum("cln,csn->cls", c_blocks, b_blocks, preferred_element_type=jnp.float32)
    weights = (scores[:, None] * decay * step_heads[:, :, None, :]).astype(jnp.bfloat16)
    inflow_scale = jnp.swapaxes(step_heads * tail, 1, 2)[..., None]
    inflow = (x_blocks * inflow_scale).astype(jnp.bfloat16)
    state = jnp.einsum("csn,cshp->chnp", b_blocks, inflow, preferred_element_type=jnp.float32)
    carried = jnp.einsum("hcd,dhnp->chnp", mixing, state, precision=HIGHEST).astype(jnp.bfloat16)
    readout = jnp.einsum("cln,chnp->clhp", c_blocks, carried, preferred_element_type=jnp.float32)
    lead_rows = jnp.swapaxes(leading, 1, 2)[..., None]
    return (
        decay,
        tail,
        mixing,
        scores,
        weights,
        inflow_scale,
        inflow,
        state,
        carried,
        readout,
        lead_rows,
    )


def mixer_parts(channels, step_raw, places, columns, biases, step_bias):
    width = step_raw.shape[1]
    length = channels.shape[0]
    spans = length // SPAN
    pre_act = convolve(channels, columns, biases, places)
    act = jax.nn.silu(pre_act).astype(jnp.bfloat16)
    x_blocks = act[:, : width * P_SIZE].reshape(spans, SPAN, width, P_SIZE)
    b_blocks = act[:, width * P_SIZE : width * P_SIZE + N].reshape(spans, SPAN, N)
    c_blocks = act[:, width * P_SIZE + N :].reshape(spans, SPAN, N)
    steps = jax.nn.softplus(step_raw.astype(jnp.float32) + step_bias)
    step_heads = jnp.swapaxes(steps.reshape(spans, SPAN, width), 1, 2)
    tables = block_tables(lax.iota(jnp.int32, length) - places)
    return (pre_act, x_blocks, b_blocks, c_blocks, step_heads, tables)


def mixer_forward(channels, step_raw, places, heads):
    columns, biases, step_bias, rates, skips = heads
    pre_act, x_blocks, b_blocks, c_blocks, step_heads, tables = mixer_parts(
        channels, step_raw, places, columns, biases, step_bias
    )
    values = scan_values(x_blocks, b_blocks, c_blocks, step_heads, rates, tables)
    weights, readout, lead_rows = (values[4], values[9], values[10])
    local = jnp.einsum("chls,cshp->clhp", weights, x_blocks, preferred_element_type=jnp.float32)
    mixed = local + readout * lead_rows + skips[None, None, :, None] * x_blocks
    return mixed.reshape(channels.shape[0], step_raw.shape[1] * P_SIZE)


def mixer_backward(grad_heads, channels, step_raw, places, heads):
    columns, biases, step_bias, rates, skips = heads
    pre_act, x_blocks, b_blocks, c_blocks, step_heads, tables = mixer_parts(
        channels, step_raw, places, columns, biases, step_bias
    )
    (
        decay,
        tail,
        mixing,
        scores,
        weights,
        inflow_scale,
        inflow,
        state,
        carried,
        readout,
        lead_rows,
    ) = scan_values(x_blocks, b_blocks, c_blocks, step_heads, rates, tables)
    between = tables[3]
    width = step_raw.shape[1]
    length = channels.shape[0]
    grad_y = grad_heads.reshape(x_blocks.shape)
    grad_float = grad_y.astype(jnp.float32)
    grad_skip = jnp.sum(grad_float * x_blocks, axis=(0, 1, 3))
    grad_x = skips[None, None, :, None] * grad_float
    grad_cumul = jnp.swapaxes(jnp.sum(grad_float * readout * lead_rows, axis=3), 1, 2)
    grad_readout = (grad_float * lead_rows).astype(jnp.bfloat16)
    grad_c = jnp.einsum("clhp,chnp->cln", grad_readout, carried, preferred_element_type=jnp.float32)
    grad_carried = jnp.einsum(
        "cln,clhp->chnp", c_blocks, grad_readout, preferred_element_type=jnp.float32
    )
    grad_state = jnp.einsum("hcd,chnp->dhnp", mixing, grad_carried, precision=HIGHEST).astype(
        jnp.bfloat16
    )
    grad_mixing = jnp.einsum("chnp,dhnp->hcd", grad_carried, state, precision=HIGHEST)
    grad_total = jnp.einsum("hcd,cdk->kh", grad_mixing * mixing, between, precision=HIGHEST)
    grad_b = jnp.einsum("cshp,chnp->csn", inflow, grad_state, preferred_element_type=jnp.float32)
    grad_inflow = jnp.einsum(
        "csn,chnp->cshp", b_blocks, grad_state, preferred_element_type=jnp.float32
    )
    grad_x = grad_x + grad_inflow * inflow_scale
    through_x = jnp.swapaxes(jnp.sum(grad_inflow * x_blocks, axis=3), 1, 2)
    grad_step = through_x * tail
    through_tail = through_x * step_heads * tail
    grad_cumul = grad_cumul - through_tail
    grad_cumul = grad_cumul.at[:, :, -1].add(jnp.sum(through_tail, axis=2) + grad_total)
    grad_weights = jnp.einsum(
        "clhp,cshp->chls", grad_y, x_blocks, preferred_element_type=jnp.float32
    )
    grad_x = grad_x + jnp.einsum(
        "chls,clhp->cshp", weights, grad_y, preferred_element_type=jnp.float32
    )
    through_decay = grad_weights * decay
    grad_scores = jnp.sum(through_decay * step_heads[:, :, None, :], axis=1).astype(jnp.bfloat16)
    with_scores = through_decay * scores[:, None]
    grad_step = grad_step + jnp.sum(with_scores, axis=2)
    paired = with_scores * step_heads[:, :, None, :]
    grad_cumul = grad_cumul + jnp.sum(paired, axis=3) - jnp.sum(paired, axis=2)
    grad_c = grad_c + jnp.einsum(
        "cls,csn->cln", grad_scores, b_blocks, preferred_element_type=jnp.float32
    )
    grad_b = grad_b + jnp.einsum(
        "cls,cln->csn", grad_scores, c_blocks, preferred_element_type=jnp.float32
    )
    grad_decay_log = jnp.flip(jnp.cumsum(jnp.flip(grad_cumul, 2), axis=2), 2)
    grad_step = grad_step + grad_decay_log * rates[None, :, None]
    grad_rate = jnp.sum(grad_decay_log * step_heads, axis=(0, 2))
    grad_act = jnp.concatenate(
        [
            grad_x.reshape(length, width * P_SIZE),
            grad_b.reshape(length, N),
            grad_c.reshape(length, N),
        ],
        1,
    )
    grad_pre = grad_act * swish_slope(pre_act)
    grad_chan, grad_columns, grad_biases = convolve_back(grad_pre, channels, columns, places)
    grad_step_raw = jnp.swapaxes(grad_step, 1, 2).reshape(length, width) * jax.nn.sigmoid(
        step_raw.astype(jnp.float32) + step_bias
    )
    head_grads = (
        grad_columns,
        grad_biases,
        jnp.sum(grad_step_raw, axis=0),
        grad_rate * rates,
        grad_skip,
    )
    return (grad_chan, grad_step_raw, head_grads)


def head_params(conv_weight, conv_bias, dt_bias, a_log, skip_d):
    width = H // lax.axis_size("seq")
    first = lax.axis_index("seq") * width
    columns = jnp.concatenate(
        [
            lax.dynamic_slice_in_dim(conv_weight, first * P_SIZE, width * P_SIZE, 1),
            conv_weight[:, DI:],
        ],
        1,
    )
    biases = jnp.concatenate(
        [lax.dynamic_slice_in_dim(conv_bias, first * P_SIZE, width * P_SIZE, 0), conv_bias[DI:]], 0
    )
    step_bias = lax.dynamic_slice_in_dim(dt_bias, first, width, 0)
    rates = -jnp.exp(lax.dynamic_slice_in_dim(a_log, first, width, 0))
    skips = lax.dynamic_slice_in_dim(skip_d, first, width, 0)
    return (columns, biases, step_bias, rates, skips)


def exchange_kernel(size, spread, src, dst, send, recv, here):
    me = lax.axis_index("seq")
    barrier = pltpu.get_barrier_semaphore()
    for distance in range(1, size):
        pl.semaphore_signal(
            barrier,
            inc=1,
            device_id={"seq": lax.rem(me + distance, size)},
            device_id_type=pl.DeviceIdType.MESH,
        )
    own = pltpu.make_async_copy(src if spread else src.at[me], dst.at[me], here)
    own.start()
    pl.semaphore_wait(barrier, size - 1)
    copies = []
    for distance in range(1, size):
        peer = lax.rem(me + distance, size)
        copy = pltpu.make_async_remote_copy(
            src_ref=src if spread else src.at[peer],
            dst_ref=dst.at[me],
            send_sem=send.at[distance - 1],
            recv_sem=recv.at[distance - 1],
            device_id={"seq": peer},
            device_id_type=pl.DeviceIdType.MESH,
        )
        copy.start()
        copies.append(copy)
    own.wait()
    for copy in copies:
        copy.wait()


def exchange(block, spread, call_id):
    size = lax.axis_size("seq")
    part = block.shape if spread else block.shape[1:]
    return pl.pallas_call(
        functools.partial(exchange_kernel, size, spread),
        out_shape=jax.ShapeDtypeStruct((size,) + part, block.dtype),
        in_specs=[pl.BlockSpec(memory_space=pltpu.VMEM)],
        out_specs=pl.BlockSpec(memory_space=pltpu.VMEM),
        scratch_shapes=[
            pltpu.SemaphoreType.DMA((size - 1,)),
            pltpu.SemaphoreType.DMA((size - 1,)),
            pltpu.SemaphoreType.DMA,
        ],
        compiler_params=pltpu.CompilerParams(
            collective_id=call_id, has_side_effects=True, vmem_limit_bytes=48 * 1024 * 1024
        ),
    )(block)


def gather_seq(block, call_id):
    return exchange(block, True, call_id).reshape((-1,) + block.shape[1:])


def swap_seq(block, call_id):
    size = lax.axis_size("seq")
    rows = block.shape[0] // size
    return exchange(block.reshape((size, rows) + block.shape[1:]), False, call_id)


SIDE = 128


def side_columns(values):
    columns = []
    for value in values:
        for _ in range(3):
            term = value.astype(jnp.bfloat16)
            columns.append(term)
            value = value - term.astype(jnp.float32)
    stacked = jnp.stack(columns, axis=1)
    return jnp.pad(stacked, ((0, 0), (0, SIDE - stacked.shape[1])))


def side_value(columns, index):
    return jnp.sum(columns[..., 3 * index : 3 * index + 3].astype(jnp.float32), axis=-1)


def input_norm(inputs, gain):
    section_in = inputs.astype(jnp.float32)
    scale = lax.rsqrt(jnp.mean(section_in * section_in, axis=-1, keepdims=True) + EPSILON)
    return (section_in, scale, (section_in * scale * gain).astype(jnp.bfloat16))


def forward_tick(inputs, places, w_in, w_out, gain, gate, heads):
    inner = w_out.shape[0]
    width = inner // P_SIZE
    normed = input_norm(gather_seq(inputs, 0), gain)[2]
    proj = jnp.dot(normed, w_in, preferred_element_type=jnp.float32)
    z_gate = proj[:, :inner]
    channels = proj[:, inner : 2 * inner + 2 * N].astype(jnp.bfloat16)
    step_raw = proj[:, 2 * inner + 2 * N : 2 * inner + 2 * N + width].astype(jnp.bfloat16)
    y_row = mixer_forward(channels, step_raw, places, heads).astype(jnp.bfloat16)
    gated = y_row.astype(jnp.float32) * jax.nn.silu(z_gate)
    part = jnp.dot((gated * gate).astype(jnp.bfloat16), w_out, preferred_element_type=jnp.float32)
    power = jnp.sum(gated * gated, axis=-1)
    parts = swap_seq(
        jnp.concatenate([part.astype(jnp.bfloat16), side_columns([power])], 1), 1
    )
    features = inputs.shape[1]
    power = jnp.sum(side_value(parts[:, :, features:], 0), axis=0)
    gate_scale = lax.rsqrt(power / DI + EPSILON)
    branch = jnp.sum(parts[:, :, :features].astype(jnp.float32), axis=0) * gate_scale[:, None]
    result = (inputs.astype(jnp.float32) + branch).astype(jnp.bfloat16)
    return (result, (inputs, normed, z_gate, channels, step_raw, y_row, gate_scale, branch, places))


def backward_tick(grad_out, kept, w_in, w_out, gain, gate, heads):
    inputs, normed, z_gate, channels, step_raw, y_row, gate_scale, branch, places = kept
    features = inputs.shape[1]
    grad_low = grad_out.astype(jnp.bfloat16)
    along = jnp.sum(grad_low.astype(jnp.float32) * branch, axis=-1)
    row = gather_seq(jnp.concatenate([grad_low, side_columns([gate_scale, along])], 1), 2)
    grad_row = row[:, :features]
    row_scale = side_value(row[:, features:], 0)[:, None]
    row_along = side_value(row[:, features:], 1)[:, None]
    grad_normed_out = lax.dot_general(
        grad_row, w_out, CONTRACT_COLS, preferred_element_type=jnp.float32
    )
    y_float = y_row.astype(jnp.float32)
    z_swish = jax.nn.silu(z_gate)
    gated = y_float * z_swish
    scaled = gated * row_scale
    normed_out = (scaled * gate).astype(jnp.bfloat16)
    grad_gate = jnp.sum(grad_normed_out * scaled, axis=0)
    grad_gated = row_scale * (grad_normed_out * gate - scaled * (row_along / DI))
    grad_y = (grad_gated * z_swish).astype(jnp.bfloat16)
    grad_z = grad_gated * y_float * swish_slope(z_gate)
    grad_chan, grad_step_raw, head_grads = mixer_backward(
        grad_y, channels, step_raw, places, heads
    )
    grad_proj = jnp.concatenate([grad_z, grad_chan, grad_step_raw], 1).astype(jnp.bfloat16)
    grad_proj = jnp.pad(grad_proj, ((0, 0), (0, w_in.shape[1] - grad_proj.shape[1])))
    part = lax.dot_general(grad_proj, w_in, CONTRACT_COLS, preferred_element_type=jnp.float32)
    grad_normed = jnp.sum(swap_seq(part.astype(jnp.bfloat16), 3).astype(jnp.float32), axis=0)
    section_in, scale, _ = input_norm(inputs, gain)
    grad_gain = jnp.sum(grad_normed * section_in * scale, axis=0)
    scaled_in = grad_normed * gain
    grad_in = grad_out + scale * (
        scaled_in
        - section_in * scale * scale * jnp.mean(scaled_in * section_in, axis=-1, keepdims=True)
    )
    smalls = (grad_gain, grad_gate) + head_grads
    return (grad_in, (normed, grad_proj), (normed_out, grad_row), smalls)


def group_columns(w_in, inner):
    me = lax.axis_index("seq")
    width = inner // P_SIZE
    parts = [
        lax.dynamic_slice_in_dim(w_in, me * inner, inner, 1),
        lax.dynamic_slice_in_dim(w_in, DI + me * inner, inner, 1),
        w_in[:, 2 * DI : 2 * DI + 2 * N],
        lax.dynamic_slice_in_dim(w_in, 2 * DI + 2 * N + me * width, width, 1),
    ]
    used = 2 * inner + 2 * N + width
    return jnp.pad(jnp.concatenate(parts, 1), ((0, 0), (0, -used % 128)))


def transposed_route(seq, wt):
    return [(s * wt + w, w * wt + s) for s in range(seq) for w in range(wt)]


def sum_small(small_totals):
    grad_gain, grad_gate, columns, biases, step_bias, rate_log, skip = small_totals
    me = lax.axis_index("seq")
    width = step_bias.shape[0]
    inner = width * P_SIZE

    def placed(member, size):
        shape = member.shape[:-1] + (size,)
        return lax.dynamic_update_slice_in_dim(
            jnp.zeros(shape, jnp.float32), member, me * member.shape[-1], member.ndim - 1
        )

    grads = [
        grad_gain,
        placed(grad_gate, DI),
        jnp.concatenate([placed(columns[:, :inner], DI), columns[:, inner:]], 1),
        jnp.concatenate([placed(biases[:inner], DI), biases[inner:]], 0),
        placed(step_bias, H),
        placed(rate_log, H),
        placed(skip, H),
    ]
    flat = lax.psum(jnp.concatenate([g.reshape(-1) for g in grads]), ("seq", "wt"))
    summed = []
    first = 0
    for grad in grads:
        summed.append(flat[first : first + grad.size].reshape(grad.shape))
        first += grad.size
    return summed


def body(
    block_input,
    positions,
    cotangent,
    norm_gain,
    in_weight,
    conv_weight,
    conv_bias,
    dt_bias,
    a_log,
    skip_d,
    gate_gain,
    out_weight,
):
    seq, wt = (lax.axis_size("seq"), lax.axis_size("wt"))
    me = lax.axis_index("seq")
    width = H // seq
    inner = width * P_SIZE
    w_in = lax.all_gather(group_columns(in_weight[0], inner), "wt", axis=0, tiled=True)
    if seq == wt:
        w_out = lax.ppermute(out_weight[0], ("seq", "wt"), transposed_route(seq, wt))
    else:
        w_out = lax.dynamic_slice_in_dim(
            lax.all_gather(out_weight[0], "wt", axis=0, tiled=True), me * inner, inner, 0
        )
    places_all = lax.all_gather(positions, "seq", axis=2, tiled=True)
    gain = norm_gain[0]
    gate = lax.dynamic_slice_in_dim(gate_gain[0], me * inner, inner, 0)
    heads = head_params(conv_weight[0], conv_bias[0], dt_bias[0], a_log[0], skip_d[0])
    first_section = lax.axis_index("section") == 0
    batches = block_input.shape[0]
    received = jnp.zeros(block_input.shape[2:], jnp.bfloat16)
    kept_ticks = []
    out_ticks = []
    for step_index in range(batches + 1):
        fresh = block_input[min(step_index, batches - 1), 0]
        inputs = jnp.where(first_section, fresh, received)
        places = jnp.where(
            first_section,
            places_all[min(step_index, batches - 1), 0],
            places_all[max(step_index - 1, 0), 0],
        )
        result, kept = forward_tick(inputs, places, w_in, w_out, gain, gate, heads)
        kept_ticks.append(kept)
        out_ticks.append(result)
        if step_index < batches:
            received = from_behind(result, "section", 1)
    grad_recv = jnp.zeros(block_input.shape[2:], jnp.float32)
    grad_ticks = []
    in_ticks = []
    out_pairs = []
    small_totals = None
    for step_index in range(batches + 1):
        if step_index < batches:
            from_loss = cotangent[step_index, 0].astype(jnp.float32)
        else:
            from_loss = jnp.zeros(block_input.shape[2:], jnp.float32)
        grad_out = jnp.where(first_section, grad_recv, from_loss)
        chosen = jax.tree.map(
            lambda early, later: jnp.where(first_section, early, later),
            kept_ticks[max(step_index - 1, 0)],
            kept_ticks[min(step_index + 1, batches)],
        )
        grad_in, in_pair, out_pair, smalls = backward_tick(
            grad_out, chosen, w_in, w_out, gain, gate, heads
        )
        grad_ticks.append(grad_in)
        in_ticks.append(in_pair)
        out_pairs.append(out_pair)
        small_totals = (
            smalls if small_totals is None else jax.tree.map(jnp.add, small_totals, smalls)
        )
        if step_index < batches:
            grad_recv = from_behind(grad_in.astype(jnp.bfloat16), "section", -1).astype(
                grad_in.dtype
            )

    def all_tokens(pairs, which):
        return jnp.concatenate(
            [
                jnp.where(first_section, pairs[index + 1][which], pairs[index][which])
                for index in range(batches)
            ]
        )

    def weight_grad(pairs):
        return lax.dot_general(
            all_tokens(pairs, 0),
            all_tokens(pairs, 1),
            CONTRACT_ROWS,
            preferred_element_type=jnp.float32,
        ).astype(jnp.bfloat16)

    grad_out_group = weight_grad(out_pairs)
    if seq == wt:
        total_out = lax.ppermute(
            lax.psum(grad_out_group, "wt"), ("seq", "wt"), transposed_route(seq, wt)
        )
    else:
        placed_out = lax.dynamic_update_slice_in_dim(
            jnp.zeros((DI, grad_out_group.shape[1]), jnp.bfloat16), grad_out_group, me * inner, 0
        )
        total_out = lax.psum(
            lax.psum_scatter(placed_out, "wt", scatter_dimension=0, tiled=True), "seq"
        )
    total_out = total_out.astype(jnp.float32)
    shard_in = lax.psum_scatter(weight_grad(in_ticks), "wt", scatter_dimension=0, tiled=True)
    groups = lax.all_gather(shard_in, "seq", axis=0)
    ends = 2 * inner + 2 * N
    total_in = jnp.concatenate(
        [groups[index, :, :inner] for index in range(seq)]
        + [groups[index, :, inner : 2 * inner] for index in range(seq)]
        + [
            jnp.sum(groups[:, :, 2 * inner : ends].astype(jnp.float32), axis=0).astype(
                jnp.bfloat16
            )
        ]
        + [groups[index, :, ends : ends + width] for index in range(seq)],
        1,
    ).astype(jnp.float32)
    summed = sum_small(small_totals)
    section_rows = jnp.stack(
        [
            jnp.where(first_section, out_ticks[index], out_ticks[index + 1])
            for index in range(batches)
        ]
    )
    grad_rows = jnp.stack(
        [
            jnp.where(first_section, grad_ticks[index + 1], grad_ticks[index])
            for index in range(batches)
        ]
    )
    return (
        section_rows[None, :, None],
        grad_rows[None, :, None],
        summed[0][None],
        total_in[None],
        summed[2][None],
        summed[3][None],
        summed[4][None],
        summed[5][None],
        summed[6][None],
        summed[1][None],
        total_out[None],
    )


def solution(mesh):
    placed = (
        P(None, "wt", "seq", None),
        P(None, "wt", "seq"),
        P(None, "wt", "seq", None),
        P("section", None),
        P("section", "wt", None),
        P("section", None, None),
        P("section", None),
        P("section", None),
        P("section", None),
        P("section", None),
        P("section", None),
        P("section", "wt", None),
    )
    return jax.shard_map(
        body,
        mesh=mesh,
        in_specs=placed,
        out_specs=(
            P("section", None, "wt", "seq", None),
            P("section", None, "wt", "seq", None),
            P("section", None),
            P("section", "wt", None),
            P("section", None, None),
            P("section", None),
            P("section", None),
            P("section", None),
            P("section", None),
            P("section", None),
            P("section", "wt", None),
        ),
        check_vma=False,
    )
```

```python
import functools

import jax
import jax.numpy as jnp
from jax import lax
from jax.experimental import pallas as pl
from jax.experimental.pallas import tpu as pltpu
from jax.sharding import PartitionSpec as P

H = 32
P_SIZE = 64
N = 128
K = 4
SPAN = 256
DI = 2048


EPSILON = 1e-05
HIGHEST = lax.Precision.HIGHEST
CONTRACT_ROWS = (((0,), (0,)), ((), ()))
CONTRACT_COLS = (((1,), (1,)), ((), ()))


def from_behind(block, axis, distance):
    devices = range(lax.axis_size(axis))
    route = [(i - distance, i) for i in devices if i - distance in devices]
    return lax.ppermute(block, axis, route)


def swish_slope(value):
    sigma = jax.nn.sigmoid(value)
    return sigma * (1.0 + value * (1.0 - sigma))


def lagged(channels, offset):
    return jnp.concatenate(
        [jnp.zeros((offset, channels.shape[1]), channels.dtype), channels[:-offset]], 0
    )


def leading_rows(channels, offset):
    return jnp.concatenate(
        [channels[offset:], jnp.zeros((offset, channels.shape[1]), channels.dtype)], 0
    )


def convolve(channels, weights, biases, places):
    values = channels.astype(jnp.float32)
    total = biases + values * weights[0]
    for offset in range(1, weights.shape[0]):
        total = total + jnp.where(
            (places >= offset)[:, None], lagged(values, offset) * weights[offset], 0.0
        )
    return total


def convolve_back(grad_pre, channels, weights, places):
    values = channels.astype(jnp.float32)
    weight_rows = [jnp.sum(grad_pre * values, axis=0)]
    grad_chan = grad_pre * weights[0]
    for offset in range(1, weights.shape[0]):
        masked = jnp.where((places >= offset)[:, None], grad_pre, 0.0)
        weight_rows.append(jnp.sum(masked * lagged(values, offset), axis=0))
        grad_chan = grad_chan + leading_rows(masked * weights[offset], offset)
    return (grad_chan, jnp.stack(weight_rows), jnp.sum(grad_pre, axis=0))


def block_tables(places):
    spans = places.shape[0] // SPAN
    local = places.reshape(spans, SPAN)
    inside = lax.iota(jnp.int32, SPAN)
    gap = inside[:, None] - inside[None, :]
    causal = (gap >= 0)[None] & (gap[None] <= local[:, :, None])
    at_end = inside[None, :] >= SPAN - 1 - local[:, -1:]
    at_start = local >= inside[None, :]
    blocks = lax.iota(jnp.int32, spans)
    between = (
        (blocks[None, :, None] < blocks[None, None, :])
        & (blocks[None, None, :] < blocks[:, None, None])
    ).astype(jnp.float32)
    across = (blocks[:, None] * SPAN - local[:, :1] < (blocks[None, :] + 1) * SPAN) & (
        blocks[None, :] < blocks[:, None]
    )
    return (causal, at_end, at_start, between, across)


def scan_values(x_blocks, b_blocks, c_blocks, step_heads, rates, tables):
    causal, at_end, at_start, between, across = tables
    cumul = jnp.cumsum(step_heads * rates[None, :, None], axis=2)
    spread = cumul[:, :, :, None] - cumul[:, :, None, :]
    inner_mask = causal[:, None]
    decay = jnp.where(inner_mask, jnp.exp(jnp.where(inner_mask, spread, 0.0)), 0.0)
    tail = jnp.where(at_end[:, None], jnp.exp(cumul[:, :, -1:] - cumul), 0.0)
    leading = jnp.where(at_start[:, None], jnp.exp(cumul), 0.0)
    segment = jnp.einsum("kh,cdk->hcd", cumul[:, :, -1], between, precision=HIGHEST)
    mixing = jnp.where(across[None], jnp.exp(jnp.where(across[None], segment, 0.0)), 0.0)
    scores = jnp.einsum("cln,csn->cls", c_blocks, b_blocks, preferred_element_type=jnp.float32)
    weights = (scores[:, None] * decay * step_heads[:, :, None, :]).astype(jnp.bfloat16)
    inflow_scale = jnp.swapaxes(step_heads * tail, 1, 2)[..., None]
    inflow = (x_blocks * inflow_scale).astype(jnp.bfloat16)
    state = jnp.einsum("csn,cshp->chnp", b_blocks, inflow, preferred_element_type=jnp.float32)
    carried = jnp.einsum("hcd,dhnp->chnp", mixing, state, precision=HIGHEST).astype(jnp.bfloat16)
    readout = jnp.einsum("cln,chnp->clhp", c_blocks, carried, preferred_element_type=jnp.float32)
    lead_rows = jnp.swapaxes(leading, 1, 2)[..., None]
    return (
        decay,
        tail,
        mixing,
        scores,
        weights,
        inflow_scale,
        inflow,
        state,
        carried,
        readout,
        lead_rows,
    )


def mixer_parts(channels, step_raw, places, columns, biases, step_bias):
    width = step_raw.shape[1]
    length = channels.shape[0]
    spans = length // SPAN
    pre_act = convolve(channels, columns, biases, places)
    act = jax.nn.silu(pre_act).astype(jnp.bfloat16)
    x_blocks = act[:, : width * P_SIZE].reshape(spans, SPAN, width, P_SIZE)
    b_blocks = act[:, width * P_SIZE : width * P_SIZE + N].reshape(spans, SPAN, N)
    c_blocks = act[:, width * P_SIZE + N :].reshape(spans, SPAN, N)
    steps = jax.nn.softplus(step_raw.astype(jnp.float32) + step_bias)
    step_heads = jnp.swapaxes(steps.reshape(spans, SPAN, width), 1, 2)
    tables = block_tables(places)
    return (pre_act, x_blocks, b_blocks, c_blocks, step_heads, tables)


def mixer_forward(channels, step_raw, places, heads):
    columns, biases, step_bias, rates, skips = heads
    pre_act, x_blocks, b_blocks, c_blocks, step_heads, tables = mixer_parts(
        channels, step_raw, places, columns, biases, step_bias
    )
    values = scan_values(x_blocks, b_blocks, c_blocks, step_heads, rates, tables)
    weights, readout, lead_rows = (values[4], values[9], values[10])
    local = jnp.einsum("chls,cshp->clhp", weights, x_blocks, preferred_element_type=jnp.float32)
    mixed = local + readout * lead_rows + skips[None, None, :, None] * x_blocks
    return mixed.reshape(channels.shape[0], step_raw.shape[1] * P_SIZE)


def mixer_backward(grad_heads, channels, step_raw, places, heads):
    columns, biases, step_bias, rates, skips = heads
    pre_act, x_blocks, b_blocks, c_blocks, step_heads, tables = mixer_parts(
        channels, step_raw, places, columns, biases, step_bias
    )
    (
        decay,
        tail,
        mixing,
        scores,
        weights,
        inflow_scale,
        inflow,
        state,
        carried,
        readout,
        lead_rows,
    ) = scan_values(x_blocks, b_blocks, c_blocks, step_heads, rates, tables)
    between = tables[3]
    width = step_raw.shape[1]
    length = channels.shape[0]
    grad_y = grad_heads.reshape(x_blocks.shape)
    grad_float = grad_y.astype(jnp.float32)
    grad_skip = jnp.sum(grad_float * x_blocks, axis=(0, 1, 3))
    grad_x = skips[None, None, :, None] * grad_float
    grad_cumul = jnp.swapaxes(jnp.sum(grad_float * readout * lead_rows, axis=3), 1, 2)
    grad_readout = (grad_float * lead_rows).astype(jnp.bfloat16)
    grad_c = jnp.einsum("clhp,chnp->cln", grad_readout, carried, preferred_element_type=jnp.float32)
    grad_carried = jnp.einsum(
        "cln,clhp->chnp", c_blocks, grad_readout, preferred_element_type=jnp.float32
    )
    grad_state = jnp.einsum("hcd,chnp->dhnp", mixing, grad_carried, precision=HIGHEST).astype(
        jnp.bfloat16
    )
    grad_mixing = jnp.einsum("chnp,dhnp->hcd", grad_carried, state, precision=HIGHEST)
    grad_total = jnp.einsum("hcd,cdk->kh", grad_mixing * mixing, between, precision=HIGHEST)
    grad_b = jnp.einsum("cshp,chnp->csn", inflow, grad_state, preferred_element_type=jnp.float32)
    grad_inflow = jnp.einsum(
        "csn,chnp->cshp", b_blocks, grad_state, preferred_element_type=jnp.float32
    )
    grad_x = grad_x + grad_inflow * inflow_scale
    through_x = jnp.swapaxes(jnp.sum(grad_inflow * x_blocks, axis=3), 1, 2)
    grad_step = through_x * tail
    through_tail = through_x * step_heads * tail
    grad_cumul = grad_cumul - through_tail
    grad_cumul = grad_cumul.at[:, :, -1].add(jnp.sum(through_tail, axis=2) + grad_total)
    grad_weights = jnp.einsum(
        "clhp,cshp->chls", grad_y, x_blocks, preferred_element_type=jnp.float32
    )
    grad_x = grad_x + jnp.einsum(
        "chls,clhp->cshp", weights, grad_y, preferred_element_type=jnp.float32
    )
    through_decay = grad_weights * decay
    grad_scores = jnp.sum(through_decay * step_heads[:, :, None, :], axis=1).astype(jnp.bfloat16)
    with_scores = through_decay * scores[:, None]
    grad_step = grad_step + jnp.sum(with_scores, axis=2)
    paired = with_scores * step_heads[:, :, None, :]
    grad_cumul = grad_cumul + jnp.sum(paired, axis=3) - jnp.sum(paired, axis=2)
    grad_c = grad_c + jnp.einsum(
        "cls,csn->cln", grad_scores, b_blocks, preferred_element_type=jnp.float32
    )
    grad_b = grad_b + jnp.einsum(
        "cls,cln->csn", grad_scores, c_blocks, preferred_element_type=jnp.float32
    )
    grad_decay_log = jnp.flip(jnp.cumsum(jnp.flip(grad_cumul, 2), axis=2), 2)
    grad_step = grad_step + grad_decay_log * rates[None, :, None]
    grad_rate = jnp.sum(grad_decay_log * step_heads, axis=(0, 2))
    grad_act = jnp.concatenate(
        [
            grad_x.reshape(length, width * P_SIZE),
            grad_b.reshape(length, N),
            grad_c.reshape(length, N),
        ],
        1,
    )
    grad_pre = grad_act * swish_slope(pre_act)
    grad_chan, grad_columns, grad_biases = convolve_back(grad_pre, channels, columns, places)
    grad_step_raw = jnp.swapaxes(grad_step, 1, 2).reshape(length, width) * jax.nn.sigmoid(
        step_raw.astype(jnp.float32) + step_bias
    )
    head_grads = (
        grad_columns,
        grad_biases,
        jnp.sum(grad_step_raw, axis=0),
        grad_rate * rates,
        grad_skip,
    )
    return (grad_chan, grad_step_raw, head_grads)


def head_params(conv_weight, conv_bias, dt_bias, a_log, skip_d):
    width = H // lax.axis_size("seq")
    first = lax.axis_index("seq") * width
    columns = jnp.concatenate(
        [
            lax.dynamic_slice_in_dim(conv_weight, first * P_SIZE, width * P_SIZE, 1),
            conv_weight[:, DI:],
        ],
        1,
    )
    biases = jnp.concatenate(
        [lax.dynamic_slice_in_dim(conv_bias, first * P_SIZE, width * P_SIZE, 0), conv_bias[DI:]], 0
    )
    step_bias = lax.dynamic_slice_in_dim(dt_bias, first, width, 0)
    rates = -jnp.exp(lax.dynamic_slice_in_dim(a_log, first, width, 0))
    skips = lax.dynamic_slice_in_dim(skip_d, first, width, 0)
    return (columns, biases, step_bias, rates, skips)


def exchange_kernel(axis, size, spread, src, dst, send, recv, here):
    me = lax.axis_index(axis)
    barrier = pltpu.get_barrier_semaphore()
    for distance in range(1, size):
        pl.semaphore_signal(
            barrier,
            inc=1,
            device_id={axis: lax.rem(me + distance, size)},
            device_id_type=pl.DeviceIdType.MESH,
        )
    own = pltpu.make_async_copy(src if spread else src.at[me], dst.at[me], here)
    own.start()
    pl.semaphore_wait(barrier, size - 1)
    copies = []
    for distance in range(1, size):
        peer = lax.rem(me + distance, size)
        copy = pltpu.make_async_remote_copy(
            src_ref=src if spread else src.at[peer],
            dst_ref=dst.at[me],
            send_sem=send.at[distance - 1],
            recv_sem=recv.at[distance - 1],
            device_id={axis: peer},
            device_id_type=pl.DeviceIdType.MESH,
        )
        copy.start()
        copies.append(copy)
    own.wait()
    for copy in copies:
        copy.wait()


def exchange(block, spread, call_id, axis="seq"):
    size = lax.axis_size(axis)
    part = block.shape if spread else block.shape[1:]
    return pl.pallas_call(
        functools.partial(exchange_kernel, axis, size, spread),
        out_shape=jax.ShapeDtypeStruct((size,) + part, block.dtype),
        in_specs=[pl.BlockSpec(memory_space=pltpu.VMEM)],
        out_specs=pl.BlockSpec(memory_space=pltpu.VMEM),
        scratch_shapes=[
            pltpu.SemaphoreType.DMA((size - 1,)),
            pltpu.SemaphoreType.DMA((size - 1,)),
            pltpu.SemaphoreType.DMA,
        ],
        compiler_params=pltpu.CompilerParams(
            collective_id=call_id, has_side_effects=True, vmem_limit_bytes=48 * 1024 * 1024
        ),
    )(block)


def gather_seq(block, call_id):
    return exchange(block, True, call_id).reshape((-1,) + block.shape[1:])


def swap_seq(block, call_id):
    size = lax.axis_size("seq")
    rows = block.shape[0] // size
    return exchange(block.reshape((size, rows) + block.shape[1:]), False, call_id)


SIDE = 128


def side_columns(values):
    columns = []
    for value in values:
        for _ in range(3):
            term = value.astype(jnp.bfloat16)
            columns.append(term)
            value = value - term.astype(jnp.float32)
    stacked = jnp.stack(columns, axis=1)
    return jnp.pad(stacked, ((0, 0), (0, SIDE - stacked.shape[1])))


def side_value(columns, index):
    return jnp.sum(columns[..., 3 * index : 3 * index + 3].astype(jnp.float32), axis=-1)


def input_norm(inputs, gain):
    section_in = inputs.astype(jnp.float32)
    scale = lax.rsqrt(jnp.mean(section_in * section_in, axis=-1, keepdims=True) + EPSILON)
    return (section_in, scale, (section_in * scale * gain).astype(jnp.bfloat16))


def forward_tick(inputs, places, w_in, w_out, gain, gate, heads):
    inner = w_out.shape[0]
    width = inner // P_SIZE
    normed = input_norm(gather_seq(inputs, 0), gain)[2]
    proj = jnp.dot(normed, w_in, preferred_element_type=jnp.float32)
    z_gate = proj[:, :inner]
    channels = proj[:, inner : 2 * inner + 2 * N].astype(jnp.bfloat16)
    step_raw = proj[:, 2 * inner + 2 * N : 2 * inner + 2 * N + width].astype(jnp.bfloat16)
    y_row = mixer_forward(channels, step_raw, places, heads).astype(jnp.bfloat16)
    gated = y_row.astype(jnp.float32) * jax.nn.silu(z_gate)
    part = jnp.dot((gated * gate).astype(jnp.bfloat16), w_out, preferred_element_type=jnp.float32)
    power = jnp.sum(gated * gated, axis=-1)
    parts = swap_seq(
        jnp.concatenate([part.astype(jnp.bfloat16), side_columns([power])], 1), 1
    )
    features = inputs.shape[1]
    power = jnp.sum(side_value(parts[:, :, features:], 0), axis=0)
    gate_scale = lax.rsqrt(power / DI + EPSILON)
    branch = jnp.sum(parts[:, :, :features].astype(jnp.float32), axis=0) * gate_scale[:, None]
    result = (inputs.astype(jnp.float32) + branch).astype(jnp.bfloat16)
    return (result, (inputs, normed, z_gate, channels, step_raw, y_row, gate_scale, branch, places))


def backward_tick(grad_out, kept, w_in, w_out, gain, gate, heads):
    inputs, normed, z_gate, channels, step_raw, y_row, gate_scale, branch, places = kept
    features = inputs.shape[1]
    grad_low = grad_out.astype(jnp.bfloat16)
    along = jnp.sum(grad_low.astype(jnp.float32) * branch, axis=-1)
    row = gather_seq(jnp.concatenate([grad_low, side_columns([gate_scale, along])], 1), 2)
    grad_row = row[:, :features]
    row_scale = side_value(row[:, features:], 0)[:, None]
    row_along = side_value(row[:, features:], 1)[:, None]
    grad_normed_out = lax.dot_general(
        grad_row, w_out, CONTRACT_COLS, preferred_element_type=jnp.float32
    )
    y_float = y_row.astype(jnp.float32)
    z_swish = jax.nn.silu(z_gate)
    gated = y_float * z_swish
    scaled = gated * row_scale
    normed_out = (scaled * gate).astype(jnp.bfloat16)
    grad_gate = jnp.sum(grad_normed_out * scaled, axis=0)
    grad_gated = row_scale * (grad_normed_out * gate - scaled * (row_along / DI))
    grad_y = (grad_gated * z_swish).astype(jnp.bfloat16)
    grad_z = grad_gated * y_float * swish_slope(z_gate)
    grad_chan, grad_step_raw, head_grads = mixer_backward(
        grad_y, channels, step_raw, places, heads
    )
    grad_proj = jnp.concatenate([grad_z, grad_chan, grad_step_raw], 1).astype(jnp.bfloat16)
    grad_proj = jnp.pad(grad_proj, ((0, 0), (0, w_in.shape[1] - grad_proj.shape[1])))
    part = lax.dot_general(grad_proj, w_in, CONTRACT_COLS, preferred_element_type=jnp.float32)
    grad_normed = jnp.sum(swap_seq(part.astype(jnp.bfloat16), 3).astype(jnp.float32), axis=0)
    section_in, scale, _ = input_norm(inputs, gain)
    grad_gain = jnp.sum(grad_normed * section_in * scale, axis=0)
    scaled_in = grad_normed * gain
    grad_in = grad_out + scale * (
        scaled_in
        - section_in * scale * scale * jnp.mean(scaled_in * section_in, axis=-1, keepdims=True)
    )
    smalls = (grad_gain, grad_gate) + head_grads
    return (grad_in, (normed, grad_proj), (normed_out, grad_row), smalls)


def group_columns(w_in, inner):
    me = lax.axis_index("seq")
    width = inner // P_SIZE
    parts = [
        lax.dynamic_slice_in_dim(w_in, me * inner, inner, 1),
        lax.dynamic_slice_in_dim(w_in, DI + me * inner, inner, 1),
        w_in[:, 2 * DI : 2 * DI + 2 * N],
        lax.dynamic_slice_in_dim(w_in, 2 * DI + 2 * N + me * width, width, 1),
    ]
    used = 2 * inner + 2 * N + width
    return jnp.pad(jnp.concatenate(parts, 1), ((0, 0), (0, -used % 128)))


def transposed_route(seq, wt):
    return [(s * wt + w, w * wt + s) for s in range(seq) for w in range(wt)]


def sum_small(small_totals):
    grad_gain, grad_gate, columns, biases, step_bias, rate_log, skip = small_totals
    me = lax.axis_index("seq")
    width = step_bias.shape[0]
    inner = width * P_SIZE

    def placed(member, size):
        shape = member.shape[:-1] + (size,)
        return lax.dynamic_update_slice_in_dim(
            jnp.zeros(shape, jnp.float32), member, me * member.shape[-1], member.ndim - 1
        )

    grads = [
        grad_gain,
        placed(grad_gate, DI),
        jnp.concatenate([placed(columns[:, :inner], DI), columns[:, inner:]], 1),
        jnp.concatenate([placed(biases[:inner], DI), biases[inner:]], 0),
        placed(step_bias, H),
        placed(rate_log, H),
        placed(skip, H),
    ]
    flat = jnp.concatenate([g.reshape(-1) for g in grads])
    flat = jnp.pad(flat, (0, -flat.shape[0] % 1024)).reshape(-1, 128)
    flat = jnp.sum(exchange(flat, True, 4, "wt"), axis=0)
    flat = jnp.sum(exchange(flat, True, 5), axis=0).reshape(-1)
    summed = []
    first = 0
    for grad in grads:
        summed.append(flat[first : first + grad.size].reshape(grad.shape))
        first += grad.size
    return summed


def body(
    block_input,
    positions,
    cotangent,
    norm_gain,
    in_weight,
    conv_weight,
    conv_bias,
    dt_bias,
    a_log,
    skip_d,
    gate_gain,
    out_weight,
):
    seq, wt = (lax.axis_size("seq"), lax.axis_size("wt"))
    me = lax.axis_index("seq")
    width = H // seq
    inner = width * P_SIZE
    w_in = lax.all_gather(group_columns(in_weight[0], inner), "wt", axis=0, tiled=True)
    if seq == wt:
        w_out = lax.ppermute(out_weight[0], ("seq", "wt"), transposed_route(seq, wt))
    else:
        w_out = lax.dynamic_slice_in_dim(
            lax.all_gather(out_weight[0], "wt", axis=0, tiled=True), me * inner, inner, 0
        )
    places_all = [
        lax.optimization_barrier(gathered.reshape(-1))
        for gathered in jnp.unstack(lax.all_gather(positions[:, 0], "seq", axis=0), axis=1)
    ]
    gain = norm_gain[0]
    gate = lax.dynamic_slice_in_dim(gate_gain[0], me * inner, inner, 0)
    heads = head_params(conv_weight[0], conv_bias[0], dt_bias[0], a_log[0], skip_d[0])
    first_section = lax.axis_index("section") == 0
    batches = block_input.shape[0]
    received = jnp.zeros(block_input.shape[2:], jnp.bfloat16)
    kept_ticks = []
    out_ticks = []
    for step_index in range(batches + 1):
        fresh = block_input[min(step_index, batches - 1), 0]
        inputs = jnp.where(first_section, fresh, received)
        places = jnp.where(
            first_section,
            places_all[min(step_index, batches - 1)],
            places_all[max(step_index - 1, 0)],
        )
        result, kept = forward_tick(inputs, places, w_in, w_out, gain, gate, heads)
        kept_ticks.append(kept)
        out_ticks.append(result)
        if step_index < batches:
            received = from_behind(result, "section", 1)
    grad_recv = jnp.zeros(block_input.shape[2:], jnp.float32)
    grad_ticks = []
    in_ticks = []
    out_pairs = []
    small_totals = None
    for step_index in range(batches + 1):
        if step_index < batches:
            from_loss = cotangent[step_index, 0].astype(jnp.float32)
        else:
            from_loss = jnp.zeros(block_input.shape[2:], jnp.float32)
        grad_out = jnp.where(first_section, grad_recv, from_loss)
        chosen = jax.tree.map(
            lambda early, later: jnp.where(first_section, early, later),
            kept_ticks[max(step_index - 1, 0)],
            kept_ticks[min(step_index + 1, batches)],
        )
        grad_in, in_pair, out_pair, smalls = backward_tick(
            grad_out, chosen, w_in, w_out, gain, gate, heads
        )
        grad_ticks.append(grad_in)
        in_ticks.append(in_pair)
        out_pairs.append(out_pair)
        small_totals = (
            smalls if small_totals is None else jax.tree.map(jnp.add, small_totals, smalls)
        )
        if step_index < batches:
            grad_recv = from_behind(grad_in.astype(jnp.bfloat16), "section", -1).astype(
                grad_in.dtype
            )

    def all_tokens(pairs, which):
        return jnp.concatenate(
            [
                jnp.where(first_section, pairs[index + 1][which], pairs[index][which])
                for index in range(batches)
            ]
        )

    def weight_grad(pairs):
        return lax.dot_general(
            all_tokens(pairs, 0),
            all_tokens(pairs, 1),
            CONTRACT_ROWS,
            preferred_element_type=jnp.float32,
        ).astype(jnp.bfloat16)

    grad_out_group = weight_grad(out_pairs)
    if seq == wt:
        total_out = lax.ppermute(
            lax.psum(grad_out_group, "wt"), ("seq", "wt"), transposed_route(seq, wt)
        )
    else:
        placed_out = lax.dynamic_update_slice_in_dim(
            jnp.zeros((DI, grad_out_group.shape[1]), jnp.bfloat16), grad_out_group, me * inner, 0
        )
        total_out = lax.psum(
            lax.psum_scatter(placed_out, "wt", scatter_dimension=0, tiled=True), "seq"
        )
    total_out = total_out.astype(jnp.float32)
    shard_in = lax.psum_scatter(weight_grad(in_ticks), "wt", scatter_dimension=0, tiled=True)
    summed = sum_small(small_totals)
    shard_in, summed = lax.optimization_barrier((shard_in, summed))
    groups = exchange(shard_in, True, 6)
    ends = 2 * inner + 2 * N
    total_in = jnp.concatenate(
        [groups[index, :, :inner] for index in range(seq)]
        + [groups[index, :, inner : 2 * inner] for index in range(seq)]
        + [
            jnp.sum(groups[:, :, 2 * inner : ends].astype(jnp.float32), axis=0).astype(
                jnp.bfloat16
            )
        ]
        + [groups[index, :, ends : ends + width] for index in range(seq)],
        1,
    ).astype(jnp.float32)
    section_rows = jnp.stack(
        [
            jnp.where(first_section, out_ticks[index], out_ticks[index + 1])
            for index in range(batches)
        ]
    )
    grad_rows = jnp.stack(
        [
            jnp.where(first_section, grad_ticks[index + 1], grad_ticks[index])
            for index in range(batches)
        ]
    )
    return (
        section_rows[None, :, None],
        grad_rows[None, :, None],
        summed[0][None],
        total_in[None],
        summed[2][None],
        summed[3][None],
        summed[4][None],
        summed[5][None],
        summed[6][None],
        summed[1][None],
        total_out[None],
    )


def solution(mesh):
    placed = (
        P(None, "wt", "seq", None),
        P(None, "wt", "seq"),
        P(None, "wt", "seq", None),
        P("section", None),
        P("section", "wt", None),
        P("section", None, None),
        P("section", None),
        P("section", None),
        P("section", None),
        P("section", None),
        P("section", None),
        P("section", "wt", None),
    )
    return jax.shard_map(
        body,
        mesh=mesh,
        in_specs=placed,
        out_specs=(
            P("section", None, "wt", "seq", None),
            P("section", None, "wt", "seq", None),
            P("section", None),
            P("section", "wt", None),
            P("section", None, None),
            P("section", None),
            P("section", None),
            P("section", None),
            P("section", None),
            P("section", None),
            P("section", "wt", None),
        ),
        check_vma=False,
    )
```
